32 devices in a mesh: replica: 4 (over y, x), shard: 8 (over z, core).
Axes of the slice: x: 2, y: 2, z: 4, core: 2. Of those that a mesh axis runs over, the one named last changes fastest.
Arguments:
- images: float32 [96, 7, 7, 512], P(('replica', 'shard')), may hold values from -6 to 6
- filters: float32 [1, 512, 4608], P(None, 'shard'), may hold values from -0.09375 to 0.09375
- out_grad: float32 [96, 7, 7, 512], P(('replica', 'shard')), may hold values from -6 to 6
Outputs:
- conv_out: float32 [96, 7, 7, 512], P(('replica', 'shard'))
- filter_grad: float32 [1, 512, 4608], P(None, 'shard', 'replica')
The draws below stay inside these ranges and needn't reach their ends.
All inputs are finite; a program needn't handle non-finite values.
Results may differ from the reference program's by a relative error of at most 0.0003.
Values sent between devices are 32-bit elements; how exact they have to be, the bound alone decides.
No kernel may reach another device: no remote copies, remote signals or barrier semaphores. Data moves between devices by JAX's collectives and lax.ppermute only.
A program may use at most 256 MiB of HBM per device.

```python
import jax
import jax.numpy as jnp
from jax import lax

GROUPS = 1
H = 7
W = 7
GW = 512
CH = 512
BATCH = 96


def block_levels(own_key, extent, cuts, smallest, largest):
    loudness, own = 1.0, jax.random.fold_in(own_key, 6)
    for position, shards_of in cuts:
        steps = jnp.exp(jax.random.uniform(jax.random.fold_in(own, position), (shards_of,), jnp.float32, smallest / len(cuts), largest / len(cuts)))
        loudness = loudness * jnp.repeat(steps, extent[position] // shards_of).reshape([-1 if axis == position else 1 for axis in range(len(extent))])
    return loudness


def centred(key, dims, deviation, bound, pieces=(), held_as=jnp.bfloat16):
    result = jax.random.normal(key, dims, jnp.float32) * deviation
    if len(pieces) > 0:
        result = block_levels(key, dims, pieces, -0.22, 0.18) * result
    return jnp.clip(result, min=-bound, max=bound).astype(held_as)


def setup_inputs(seed: int = 0) -> dict:
    key_list = jax.random.split(jax.random.key(seed), 4)
    return {
        "images": centred(key_list[0], (BATCH, H, W, CH), 1.0, 6.0, ((0, 32),), jnp.float32),
        "filters": centred(key_list[1], (GROUPS, GW, 9 * GW), (9 * GW) ** -0.5, 0.09375, ((1, 8),), jnp.float32),
        "out_grad": centred(key_list[2], (BATCH, H, W, CH), 1.0, 6.0, ((0, 32),), jnp.float32),
    }


def conv_patches(block):
    batch, rows, cols, chans = block.shape
    padded = jnp.pad(block, ((0, 0), (1, 1), (1, 1), (0, 0)))
    taps = [padded[:, a:a + rows, c:c + cols, :] for a in range(3) for c in range(3)]
    return jnp.concatenate(taps, axis=3).reshape(batch * rows * cols, 9 * chans)


def reference(images, filters, out_grad):
    batch, rows, cols, chans = images.shape
    width = filters.shape[1]
    count = filters.shape[0]

    def one_group(group):
        start = (group * width).astype(jnp.int32)
        patch = conv_patches(lax.dynamic_slice_in_dim(images, start, width, 3))
        grad_rows = lax.dynamic_slice_in_dim(out_grad, start, width, 3).reshape(-1, width)
        weight = lax.dynamic_index_in_dim(filters, group, 0, keepdims=False)
        output = lax.dot_general(patch, weight, (((1,), (1,)), ((), ())), precision=lax.Precision.HIGHEST, preferred_element_type=jnp.float32)
        grads = lax.dot_general(grad_rows, patch, (((0,), (0,)), ((), ())), precision=lax.Precision.HIGHEST, preferred_element_type=jnp.float32)
        return output, grads

    outputs, grads = lax.map(one_group, jnp.arange(count, dtype=jnp.int32))
    conv_out = jnp.transpose(outputs, (1, 0, 2)).reshape(batch, rows, cols, chans)
    return conv_out, grads
```

```python
import functools

import jax
import jax.numpy as jnp
from jax import lax
from jax.experimental import pallas as pl
from jax.experimental.pallas import tpu as pltpu
from jax.sharding import PartitionSpec as P

CORES = 2
LANES = 128
VMEM_BYTES = 48 * 1024 * 1024
VMEM = pl.BlockSpec(memory_space=pltpu.VMEM)
SMEM = pl.BlockSpec(memory_space=pltpu.SMEM)


def params():
    return pltpu.CompilerParams(vmem_limit_bytes=VMEM_BYTES)


def slot_of(owner, rep, count):
    if count & (count - 1):
        return lax.rem(owner - rep + count, count)
    return jnp.bitwise_xor(jnp.int32(owner), rep)


def partner(rep, step, count):
    if count & (count - 1):
        return (rep + step) % count
    return rep ^ step


def split_kernel(parts, ids, grad_ref, *out_refs):
    wide = out_refs[0].shape[-1]
    for d in range(parts):
        start = lax.rem(ids[0] + d, parts) * wide
        out_refs[d][...] = grad_ref[:, :, :, pl.ds(pl.multiple_of(start, wide), wide)]


def join_kernel(parts, ids, *refs):
    out_ref = refs[-1]
    wide = refs[0].shape[-1]
    for d in range(parts):
        start = lax.rem(ids[0] + parts - d, parts) * wide
        out_ref[:, :, :, pl.ds(pl.multiple_of(start, wide), wide)] = refs[d][...]


def halves(value):
    high = value.astype(jnp.bfloat16)
    low = (value - high.astype(jnp.float32)).astype(jnp.bfloat16)
    return high, low


def filter_kernel(ids, own_ref, mate_ref, high_ref, low_ref):
    owned, kdim = own_ref.shape[1:]
    width = kdim // 9
    first = ids[1] == 0
    for tap in range(9):
        own = own_ref[0, :, tap * width : (tap + 1) * width]
        mate = mate_ref[0, :, tap * width : (tap + 1) * width]
        both = jnp.concatenate(
            [jnp.where(first, own, mate), jnp.where(first, mate, own)], axis=0
        )
        rows = slice(tap * 2 * owned, (tap + 1) * 2 * owned)
        high_ref[rows, :], low_ref[rows, :] = halves(both)


def grad_kernel(*refs):
    *in_refs, high_ref, low_ref, pad_ref = refs
    count, rows, cols, wide = in_refs[0].shape
    line = 8
    block = (rows + 2) * line
    images = len(in_refs) * count
    pad_ref[...] = jnp.zeros_like(pad_ref)
    for j, ref in enumerate(in_refs):
        for b in range(count):
            for h in range(rows):
                at = 8 + (j * count + b) * block + (h + 1) * line
                pad_ref[at : at + cols, :] = ref[j * 0 + b, h]
    spare = high_ref.shape[1] - images * rows * line
    for a in range(3):
        for c in range(3):
            tap = 3 * a + c
            pieces = []
            for image in range(images):
                start = 8 + image * block + (2 - a) * line - (c - 1)
                pieces.append(pad_ref[start : start + rows * line, :])
            if spare:
                pieces.append(jnp.zeros((spare, wide), jnp.float32))
            turned = jnp.transpose(jnp.concatenate(pieces, axis=0))
            out = slice(tap * wide, (tap + 1) * wide)
            high_ref[out, :], low_ref[out, :] = halves(turned)


def dot_nt(lhs, rhs):
    return lax.dot_general(
        lhs, rhs, (((1,), (1,)), ((), ())), preferred_element_type=jnp.float32
    )


def dot_nn(lhs, rhs):
    return lax.dot_general(
        lhs, rhs, (((1,), (0,)), ((), ())), preferred_element_type=jnp.float32
    )


def main_kernel(parts, replicas, ids, *refs):
    x_refs = refs[:parts]
    wh_ref, wl_ref, gh_ref, gl_ref = refs[parts : parts + 4]
    conv_refs = refs[parts + 4 : 2 * parts + 4]
    own_ref, mate_ref, rows_ref, y_ref = refs[2 * parts + 4 :]
    count, height, cols, width = x_refs[0].shape
    line = 8
    block = height * line
    images = parts * count
    real = images * block
    wide = conv_refs[0].shape[-1]
    owned = wide // CORES
    span = own_ref.shape[-1]
    rep = ids[2]
    first = ids[1] == 0

    rows_ref[...] = jnp.zeros_like(rows_ref)
    for j, ref in enumerate(x_refs):
        for b in range(count):
            for h in range(height):
                at = (j * count + b) * block + h * line
                rows_ref[at : at + cols, :] = ref[b, h]
    xh, xl = halves(rows_ref[...])

    for tap in range(9):
        out = slice(tap * wide, (tap + 1) * wide)
        gh = gh_ref[out, :]
        total = dot_nn(gh, xh) + dot_nn(gh, xl) + dot_nn(gl_ref[out, :], xh)
        top, bottom = total[:owned], total[owned:]
        own = jnp.where(first, top, bottom)
        mate = jnp.where(first, bottom, top)
        for unit in range(width // LANES):
            lane = tap * width + unit * LANES
            slot = slot_of(lane // span, rep, replicas)
            at = lane % span
            lanes = slice(unit * LANES, (unit + 1) * LANES)
            own_ref[slot, :, at : at + LANES] = own[:, lanes]
            mate_ref[slot, :, at : at + LANES] = mate[:, lanes]

    xh, xl = xh[:real], xl[:real]
    step = 2 * wide
    for start in range(0, 9 * wide, step):
        out = slice(start, min(start + step, 9 * wide))
        wh = wh_ref[out, :]
        y_ref[:, out] = dot_nt(xh, wh) + dot_nt(xl, wh) + dot_nt(xh, wl_ref[out, :])
    gap = jnp.zeros((line, wide), jnp.float32)
    for j in range(parts):
        for b in range(count):
            at = (j * count + b) * block
            sums = []
            for c in range(3):
                above, middle, below = (
                    y_ref[at : at + block, (3 * a + c) * wide : (3 * a + c + 1) * wide]
                    for a in range(3)
                )
                sums.append(
                    middle
                    + jnp.concatenate([gap, above[:-line]], axis=0)
                    + jnp.concatenate([below[line:], gap], axis=0)
                )
            result = (
                sums[1]
                + pltpu.roll(sums[0], 1, axis=0)
                + pltpu.roll(sums[2], block - 1, axis=0)
            )
            for h in range(height):
                conv_refs[j][b, h] = result[h * line : h * line + cols]


def on_device(images, filters, out_grad):
    count, rows, cols, chans = images.shape
    owned, kdim = filters.shape[1:]
    width = kdim // 9
    shards, replicas = lax.axis_size("shard"), lax.axis_size("replica")
    parts = shards // CORES
    wide = owned * CORES
    span = kdim // replicas
    shard, rep = lax.axis_index("shard"), lax.axis_index("replica")
    ids = jnp.stack([shard // CORES, shard % CORES, rep]).astype(jnp.int32)
    f32 = functools.partial(jax.ShapeDtypeStruct, dtype=jnp.float32)
    bf16 = functools.partial(jax.ShapeDtypeStruct, dtype=jnp.bfloat16)

    def onward(value, d):
        return lax.ppermute(
            value, "shard", [(s, (s + CORES * d) % shards) for s in range(shards)]
        )

    def across(value):
        return lax.ppermute(value, "shard", [(s, s ^ 1) for s in range(shards)])

    mate_filters = across(filters)
    image_blocks = [images] + [onward(images, parts - d) for d in range(1, parts)]

    small = f32((count, rows, cols, wide))
    grad_parts = pl.pallas_call(
        functools.partial(split_kernel, parts),
        out_shape=[small] * parts,
        in_specs=[SMEM, VMEM],
        out_specs=[VMEM] * parts,
        compiler_params=params(),
        name="split_grad",
    )(ids, out_grad)
    grad_blocks = [grad_parts[0]] + [
        onward(grad_parts[parts - d], parts - d) for d in range(1, parts)
    ]

    wh, wl = pl.pallas_call(
        filter_kernel,
        out_shape=[bf16((9 * wide, width))] * 2,
        in_specs=[SMEM, VMEM, VMEM],
        out_specs=[VMEM] * 2,
        compiler_params=params(),
        name="prepare_filters",
    )(ids, filters, mate_filters)

    real = parts * count * rows * 8
    depth = -(-real // LANES) * LANES
    gh, gl = pl.pallas_call(
        grad_kernel,
        out_shape=[bf16((9 * wide, depth))] * 2,
        in_specs=[VMEM] * parts,
        out_specs=[VMEM] * 2,
        scratch_shapes=[pltpu.VMEM((16 + parts * count * (rows + 2) * 8, wide), jnp.float32)],
        compiler_params=params(),
        name="prepare_grad",
    )(*grad_blocks)

    *conv_parts, grad_own, grad_mate = pl.pallas_call(
        functools.partial(main_kernel, parts, replicas),
        out_shape=[small] * parts + [f32((replicas, owned, span))] * 2,
        in_specs=[SMEM] + [VMEM] * (parts + 4),
        out_specs=[VMEM] * (parts + 2),
        scratch_shapes=[
            pltpu.VMEM((depth, width), jnp.float32),
            pltpu.VMEM((real, 9 * wide), jnp.float32),
        ],
        compiler_params=params(),
        name="multiply",
    )(ids, *image_blocks, wh, wl, gh, gl)

    total = grad_own + across(grad_mate)
    filter_grad = total[0]
    for step in range(1, replicas):
        filter_grad = filter_grad + lax.ppermute(
            total[step],
            "replica",
            [(r, partner(r, step, replicas)) for r in range(replicas)],
        )

    returned = [conv_parts[0]] + [onward(conv_parts[d], d) for d in range(1, parts)]
    conv_out = pl.pallas_call(
        functools.partial(join_kernel, parts),
        out_shape=f32(images.shape),
        in_specs=[SMEM] + [VMEM] * parts,
        out_specs=VMEM,
        compiler_params=params(),
        name="join_output",
    )(ids, *returned)
    return conv_out, filter_grad[None]


def solution(mesh):
    return jax.shard_map(
        on_device,
        mesh=mesh,
        in_specs=(
            P(("replica", "shard"), None, None, None),
            P(None, "shard", None),
            P(("replica", "shard"), None, None, None),
        ),
        out_specs=(P(("replica", "shard"), None, None, None), P(None, "shard", "replica")),
        check_vma=False,
    )
```

```python
import functools

import jax
import jax.numpy as jnp
from jax import lax
from jax.experimental import pallas as pl
from jax.experimental.pallas import tpu as pltpu
from jax.sharding import PartitionSpec as P

CORES = 2
LANES = 128
LINE = 8
CHUNK_SHARES = (3, 1)
VMEM = pl.BlockSpec(memory_space=pltpu.VMEM)
SMEM = pl.BlockSpec(memory_space=pltpu.SMEM)


def params(mib=24):
    return pltpu.CompilerParams(vmem_limit_bytes=mib * 1024 * 1024)


def chunk_units(width):
    units = width // LANES
    share = units // sum(CHUNK_SHARES)
    bounds = [0]
    for part in CHUNK_SHARES:
        bounds.append(bounds[-1] + part * share)
    bounds[-1] = units
    return [list(range(a, b)) for a, b in zip(bounds, bounds[1:])]


def exchange_plan(width, replicas):
    units = width // LANES
    span = 9 * units // replicas
    chunks = chunk_units(width)
    late = [[] for _ in range(replicas)]
    plan = []
    for index, chunk in enumerate(chunks):
        mine = [
            [(t, u) for t in range(9) for u in chunk if (t * units + u) // span == q]
            for q in range(replicas)
        ]
        if index + 1 < len(chunks):
            base = min(len(m) for m in mine)
            for q in range(replicas):
                late[q] += mine[q][base:]
                mine[q] = mine[q][:base]
        else:
            mine = [m + extra for m, extra in zip(mine, late)]
        plan.append(mine)
    return plan


def halves(value):
    high = value.astype(jnp.bfloat16)
    low = (value - high.astype(jnp.float32)).astype(jnp.bfloat16)
    return high, low


def dot_nt(lhs, rhs):
    return lax.dot_general(
        lhs, rhs, (((1,), (1,)), ((), ())), preferred_element_type=jnp.float32
    )


def dot_nn(lhs, rhs):
    return lax.dot_general(
        lhs, rhs, (((1,), (0,)), ((), ())), preferred_element_type=jnp.float32
    )


def pack_kernel(chunks, image_ref, grad_ref, *out_refs):
    *chunk_refs, split_ref = out_refs
    count, rows, cols, width = image_ref.shape
    dense = count * rows * cols
    spare = split_ref.shape[1] - dense
    sources = [(image_ref, ref, units) for ref, units in zip(chunk_refs, chunks)]
    sources.append((grad_ref, split_ref, list(range(width // LANES))))
    for src, ref, units in sources:
        for p, unit in enumerate(units):
            lanes = slice(unit * LANES, (unit + 1) * LANES)
            for b in range(count):
                for h in range(rows):
                    at = (b * rows + h) * cols
                    ref[p, at : at + cols, :] = src[b, h, :, lanes]
            if spare:
                ref[p, dense:, :] = jnp.zeros((spare, LANES), jnp.float32)


def join_kernel(in_ref, out_ref):
    count, rows, cols, width = out_ref.shape
    for p in range(width // LANES):
        lanes = slice(p * LANES, (p + 1) * LANES)
        for b in range(count):
            for h in range(rows):
                at = (b * rows + h) * cols
                out_ref[b, h, :, lanes] = in_ref[p, at : at + cols, :]


def filter_kernel(chunks, ids, own_ref, mate_ref, *out_refs):
    owned, kdim = own_ref.shape[1:]
    width = kdim // 9
    first = ids[1] == 0
    for tap in range(9):
        rows = slice(tap * 2 * owned, (tap + 1) * 2 * owned)
        for ref, units in zip(out_refs, chunks):
            size = len(units) * LANES
            at = tap * width + units[0] * LANES
            own = own_ref[0, :, at : at + size]
            mate = mate_ref[0, :, at : at + size]
            both = jnp.concatenate(
                [jnp.where(first, own, mate), jnp.where(first, mate, own)], axis=0
            )
            high, low = halves(both)
            ref[rows, :size] = high
            ref[rows, size : 2 * size] = high
            ref[rows, 2 * size :] = low


def grad_kernel(count, rows, cols, ids, in_ref, high_ref, low_ref, pad_ref):
    parts = in_ref.shape[0]
    block = (rows + 2) * LINE
    images = parts * count
    pad_ref[...] = jnp.zeros_like(pad_ref)
    for j in range(parts):
        source = lax.rem(ids[0] + j, parts)
        for b in range(count):
            for h in range(rows):
                at = LINE + (j * count + b) * block + (h + 1) * LINE
                dense = (b * rows + h) * cols
                pad_ref[at : at + cols, :] = in_ref[source, dense : dense + cols, :]
    spare = high_ref.shape[1] - images * rows * LINE
    for a in range(3):
        for c in range(3):
            tap = 3 * a + c
            pieces = []
            for image in range(images):
                start = LINE + image * block + (2 - a) * LINE - (c - 1)
                pieces.append(pad_ref[start : start + rows * LINE, :])
            if spare:
                pieces.append(jnp.zeros((spare, LANES), jnp.float32))
            turned = jnp.transpose(jnp.concatenate(pieces, axis=0))
            out = slice(tap * LANES, (tap + 1) * LANES)
            high_ref[out, :], low_ref[out, :] = halves(turned)


def main_kernel(parts, shape, chunk, plan, late, last, ids, *refs):
    refs = list(refs)
    take = lambda k: [refs.pop(0) for _ in range(k)]
    x_refs = take(parts)
    w_ref, gh_ref, gl_ref = take(3)
    before_ref = take(1)[0] if chunk[0] else None
    extra_refs = take(len(late)) if last else []
    conv_ref, own_ref, mate_ref = take(3)
    extra_out = take(1)[0] if not last and late else None
    rows_ref, y_ref = take(2)
    count, height, cols = shape
    block = height * LINE
    images = parts * count
    real = images * block
    size = len(chunk) * LANES
    first = ids[1] == 0

    rows_ref[...] = jnp.zeros_like(rows_ref)
    for j, ref in enumerate(x_refs):
        for p in range(len(chunk)):
            for line in range(count * height):
                at = (j * count * height + line) * LINE
                rows_ref[at : at + cols, p * LANES : (p + 1) * LANES] = ref[
                    p, line * cols : (line + 1) * cols, :
                ]
    xh, xl = halves(rows_ref[...])
    sides = jnp.concatenate([xh, xl], axis=1)

    places = {pair: (q, i) for q, pairs in enumerate(plan) for i, pair in enumerate(pairs)}

    def keep(slot, at, value):
        top, bottom = value[: LANES // CORES], value[LANES // CORES :]
        lanes = slice(at * LANES, (at + 1) * LANES)
        own_ref[slot, :, lanes] = jnp.where(first, top, bottom)
        mate_ref[slot, :, lanes] = jnp.where(first, bottom, top)

    spared = 0
    for tap in range(9):
        out = slice(tap * LANES, (tap + 1) * LANES)
        wide = dot_nn(gh_ref[out, :], sides)
        total = wide[:, :size] + wide[:, size:] + dot_nn(gl_ref[out, :], xh)
        for p, unit in enumerate(chunk):
            value = total[:, p * LANES : (p + 1) * LANES]
            if (tap, unit) in places:
                keep(*places[tap, unit], value)
            else:
                extra_out[spared] = value
                spared += 1
    for ref, pairs in zip(extra_refs, late):
        for i, pair in enumerate(pairs):
            keep(*places[pair], ref[i])

    packed = jnp.concatenate([xh, xl, xh], axis=1)[:real]
    for start in range(0, 9 * LANES, 2 * LANES):
        out = slice(start, min(start + 2 * LANES, 9 * LANES))
        y_ref[:, out] = dot_nt(packed, w_ref[out, :])
    gap = jnp.zeros((LINE, LANES), jnp.float32)
    for j in range(parts):
        target = lax.rem(ids[0] + j, parts)
        for b in range(count):
            at = (j * count + b) * block
            sums = []
            for c in range(3):
                above, middle, below = (
                    y_ref[at : at + block, (3 * a + c) * LANES : (3 * a + c + 1) * LANES]
                    for a in range(3)
                )
                sums.append(
                    middle
                    + jnp.concatenate([gap, above[:-LINE]], axis=0)
                    + jnp.concatenate([below[LINE:], gap], axis=0)
                )
            result = (
                sums[1]
                + pltpu.roll(sums[0], 1, axis=0)
                + pltpu.roll(sums[2], block - 1, axis=0)
            )
            if before_ref is not None:
                result = result + before_ref[at : at + block, :]
            if not last:
                conv_ref[at : at + block, :] = result
            else:
                for h in range(height):
                    dense = (b * height + h) * cols
                    conv_ref[target, dense : dense + cols, :] = result[
                        h * LINE : h * LINE + cols
                    ]
        spare = conv_ref.shape[1] - count * height * cols
        if last and spare:
            conv_ref[target, count * height * cols :, :] = jnp.zeros(
                (spare, LANES), jnp.float32
            )


def sum_kernel(plan, width, replicas, ids, *refs):
    *in_refs, out_ref = refs
    span = out_ref.shape[-1]
    for ref, owners in zip(in_refs, plan):
        for i in range(len(owners[0])):
            lanes = slice(i * LANES, (i + 1) * LANES)
            value = ref[0, :, lanes]
            for r in range(1, replicas):
                value = value + ref[r, :, lanes]
            place = jnp.int32(0)
            for q, pairs in enumerate(owners):
                tap, unit = pairs[i]
                place = jnp.where(ids[2] == q, tap * width + unit * LANES - q * span, place)
            out_ref[0, :, pl.ds(pl.multiple_of(place, LANES), LANES)] = value


def on_device(images, filters, out_grad):
    count, rows, cols, chans = images.shape
    owned, kdim = filters.shape[1:]
    width = kdim // 9
    shards, replicas = lax.axis_size("shard"), lax.axis_size("replica")
    parts = shards // CORES
    span = kdim // replicas
    shard, rep = lax.axis_index("shard"), lax.axis_index("replica")
    ids = jnp.stack([shard // CORES, shard % CORES, rep]).astype(jnp.int32)
    f32 = functools.partial(jax.ShapeDtypeStruct, dtype=jnp.float32)
    bf16 = functools.partial(jax.ShapeDtypeStruct, dtype=jnp.bfloat16)
    chunks = chunk_units(width)
    plan = exchange_plan(width, replicas)
    lines = [[s for s in range(shards) if s % CORES == core] for core in range(CORES)]

    def onward(value, d):
        return lax.ppermute(
            value, "shard", [(s, (s + CORES * d) % shards) for s in range(shards)]
        )

    def across(value):
        return lax.ppermute(value, "shard", [(s, s ^ 1) for s in range(shards)])

    def gather(value):
        blocks = [value] + [None] * (parts - 1)
        up = down = value
        for step in range(1, parts // 2 + 1):
            up = onward(up, 1)
            blocks[parts - step] = up
            if step <= (parts - 1) // 2:
                down = onward(down, -1)
                blocks[step] = down
        return blocks

    mate_filters = across(filters)

    packed = -(-count * rows * cols // 8) * 8
    *image_chunks, grad_split = pl.pallas_call(
        functools.partial(pack_kernel, chunks),
        out_shape=[f32((len(c), packed, LANES)) for c in chunks]
        + [f32((parts, packed, LANES))],
        in_specs=[VMEM] * 2,
        out_specs=[VMEM] * (len(chunks) + 1),
        compiler_params=params(),
        name="pack",
    )(images, out_grad)
    gathered = [gather(chunk) for chunk in image_chunks]
    grad_parts = lax.all_to_all(
        grad_split, "shard", 0, 0, axis_index_groups=lines, tiled=True
    )

    weights = pl.pallas_call(
        functools.partial(filter_kernel, chunks),
        out_shape=[bf16((9 * LANES, 3 * len(c) * LANES)) for c in chunks],
        in_specs=[SMEM, VMEM, VMEM],
        out_specs=[VMEM] * len(chunks),
        compiler_params=params(),
        name="prepare_filters",
    )(ids, filters, mate_filters)

    real = parts * count * rows * LINE
    depth = -(-real // LANES) * LANES
    gh, gl = pl.pallas_call(
        functools.partial(grad_kernel, count, rows, cols),
        out_shape=[bf16((9 * LANES, depth))] * 2,
        in_specs=[SMEM, VMEM],
        out_specs=[VMEM] * 2,
        scratch_shapes=[
            pltpu.VMEM((2 * LINE + parts * count * (rows + 2) * LINE, LANES), jnp.float32)
        ],
        compiler_params=params(),
        name="prepare_grad",
    )(ids, grad_parts)

    conv = None
    extras, late, sums = [], [], []
    for index, chunk in enumerate(chunks):
        last = index + 1 == len(chunks)
        carried = {pair for pairs in plan[index] for pair in pairs}
        spare = [(t, u) for t in range(9) for u in chunk if (t, u) not in carried]
        size = len(chunk) * LANES
        blocks = [f32((replicas, owned, len(plan[index][0]) * LANES))] * 2
        out_shape = [f32((parts, packed, LANES) if last else (real, LANES))] + blocks
        if not last and spare:
            out_shape.append(f32((len(spare), LANES, LANES)))
        operands = [*gathered[index], weights[index], gh, gl]
        if index:
            operands.append(conv)
        if last:
            operands += extras
        conv, own, mate, *spared = pl.pallas_call(
            functools.partial(
                main_kernel,
                parts,
                (count, rows, cols),
                chunk,
                plan[index],
                late if last else spare,
                last,
            ),
            out_shape=out_shape,
            in_specs=[SMEM] + [VMEM] * len(operands),
            out_specs=[VMEM] * len(out_shape),
            scratch_shapes=[
                pltpu.VMEM((depth, size), jnp.float32),
                pltpu.VMEM((real, 9 * LANES), jnp.float32),
            ],
            compiler_params=params(),
            name="multiply",
        )(ids, *operands)
        if not last and spare:
            extras += spared
            late.append(spare)
        sums.append(
            lax.all_to_all(own + across(mate), "replica", 0, 0, tiled=True)
        )

    returned = lax.all_to_all(conv, "shard", 0, 0, axis_index_groups=lines, tiled=True)
    conv_out = pl.pallas_call(
        join_kernel,
        out_shape=f32(images.shape),
        in_specs=[VMEM],
        out_specs=VMEM,
        compiler_params=params(),
        name="join_output",
    )(returned)
    filter_grad = pl.pallas_call(
        functools.partial(sum_kernel, plan, width, replicas),
        out_shape=f32((1, owned, span)),
        in_specs=[SMEM] + [VMEM] * len(sums),
        out_specs=VMEM,
        compiler_params=params(),
        name="sum_replicas",
    )(ids, *sums)
    return conv_out, filter_grad


def solution(mesh):
    return jax.shard_map(
        on_device,
        mesh=mesh,
        in_specs=(
            P(("replica", "shard"), None, None, None),
            P(None, "shard", None),
            P(("replica", "shard"), None, None, None),
        ),
        out_specs=(P(("replica", "shard"), None, None, None), P(None, "shard", "replica")),
        check_vma=False,
    )
```

```python
import functools

import jax
import jax.numpy as jnp
from jax import lax
from jax.experimental import pallas as pl
from jax.experimental.pallas import tpu as pltpu
from jax.sharding import PartitionSpec as P

CORES = 2
LANES = 128
LINE = 8
CHUNK_SHARES = (2, 2)
VMEM = pl.BlockSpec(memory_space=pltpu.VMEM)
SMEM = pl.BlockSpec(memory_space=pltpu.SMEM)


def call(kernel, name, out_shape, operands, scratch=(), mib=24):
    return pl.pallas_call(
        kernel,
        out_shape=out_shape,
        in_specs=[SMEM] + [VMEM] * (len(operands) - 1),
        out_specs=[VMEM] * len(out_shape),
        scratch_shapes=list(scratch),
        compiler_params=pltpu.CompilerParams(vmem_limit_bytes=mib * 1024 * 1024),
        cost_estimate=pl.CostEstimate(flops=0, bytes_accessed=0, transcendentals=0),
        name=name,
    )(*operands)


def chunk_units(width):
    units = width // LANES
    share = units // sum(CHUNK_SHARES)
    bounds = [0]
    for part in CHUNK_SHARES:
        bounds.append(bounds[-1] + part * share)
    bounds[-1] = units
    return [list(range(a, b)) for a, b in zip(bounds, bounds[1:])]


def exchange_plan(width, replicas):
    units = width // LANES
    span = 9 * units // replicas
    chunks = chunk_units(width)
    late = [[] for _ in range(replicas)]
    plan = []
    for index, chunk in enumerate(chunks):
        mine = [
            [(t, u) for t in range(9) for u in chunk if (t * units + u) // span == q]
            for q in range(replicas)
        ]
        if index + 1 < len(chunks):
            base = min(len(m) for m in mine)
            for q in range(replicas):
                late[q] += mine[q][base:]
                mine[q] = mine[q][:base]
        else:
            mine = [m + extra for m, extra in zip(mine, late)]
        plan.append(mine)
    return plan


def partner(rep, step, count):
    return (rep + step) % count if count & (count - 1) else rep ^ step


def slot_of(owner, rep, count):
    if count & (count - 1):
        return lax.rem(owner - rep + count, count)
    return jnp.bitwise_xor(jnp.int32(owner), rep)


def after(value, *others):
    return lax.optimization_barrier((value, *others))[0]


def split(value):
    high = value.astype(jnp.bfloat16).astype(jnp.float32)
    return high, value - high


def deep_rows(first, second, third):
    rows, lanes = first.shape
    full = rows // LANES * LANES
    pieces = [p[:full] for p in (first, second, third)] if full else []
    rest = 3 * (rows - full)
    if rest:
        pieces += [p[full:] for p in (first, second, third)]
        gap = -rest % LANES
        if gap:
            pieces.append(jnp.zeros((gap, lanes), jnp.float32))
    return jnp.concatenate(pieces, axis=0)


def dot_nt(lhs, rhs):
    return lax.dot_general(
        lhs, rhs, (((1,), (1,)), ((), ())), preferred_element_type=jnp.float32
    )


def dot_nn(lhs, rhs):
    return lax.dot_general(
        lhs, rhs, (((1,), (0,)), ((), ())), preferred_element_type=jnp.float32
    )


def pack_kernel(chunks, parts, ids, image_ref, grad_ref, *refs):
    up_ref, down_ref, *chunk_refs, own_ref = refs
    count, rows, cols, width = image_ref.shape
    dense = count * rows * cols
    spare = own_ref.shape[1] - dense

    def pack(src, lanes, targets):
        for b in range(count):
            for h in range(rows):
                at = (b * rows + h) * cols
                value = src[b, h, :, lanes]
                for ref, p in targets:
                    ref[p, at : at + cols, :] = value
        if spare:
            for ref, p in targets:
                ref[p, dense:, :] = jnp.zeros((spare, LANES), jnp.float32)

    for p, unit in enumerate(chunks[0]):
        pack(image_ref, pl.ds(unit * LANES, LANES), [(up_ref, p), (down_ref, p)])
    for ref, units in zip(chunk_refs, chunks[1:]):
        for p, unit in enumerate(units):
            pack(image_ref, pl.ds(unit * LANES, LANES), [(ref, p)])
    for d in range(parts):
        start = ids[2 + d] * LANES
        if d == 0:
            target = (own_ref, 0)
        elif d <= parts // 2:
            target = (up_ref, up_ref.shape[0] - d)
        else:
            target = (down_ref, down_ref.shape[0] - (parts - d))
        pack(grad_ref, pl.ds(pl.multiple_of(start, LANES), LANES), [target])


def join_kernel(parts, ids, *refs):
    out_ref = refs[-1]
    count, rows, cols, width = out_ref.shape
    for d in range(parts):
        start = ids[2 + (parts - d) % parts] * LANES
        lanes = pl.ds(pl.multiple_of(start, LANES), LANES)
        for b in range(count):
            for h in range(rows):
                at = (b * rows + h) * cols
                out_ref[b, h, :, lanes] = refs[d][at : at + cols, :]


def filter_kernel(chunks, ids, own_ref, mate_ref, *out_refs):
    owned, kdim = own_ref.shape[1:]
    width = kdim // 9
    first = ids[0] == 0
    for tap in range(9):
        rows = slice(tap * 2 * owned, (tap + 1) * 2 * owned)
        for ref, units in zip(out_refs, chunks):
            size = len(units) * LANES
            at = tap * width + units[0] * LANES
            own = own_ref[0, :, at : at + size]
            mate = mate_ref[0, :, at : at + size]
            both = jnp.concatenate(
                [jnp.where(first, own, mate), jnp.where(first, mate, own)], axis=0
            )
            high, low = split(both)
            high = high.astype(jnp.bfloat16)
            ref[rows, :size] = high
            ref[rows, size : 2 * size] = high
            ref[rows, 2 * size :] = low.astype(jnp.bfloat16)


def grad_kernel(shape, ids, *refs):
    count, rows, cols = shape
    *refs, pad_ref = refs
    in_refs, out_refs = refs[: len(refs) // 2], refs[len(refs) // 2 :]
    block = (rows + 2) * LINE
    pad_ref[...] = jnp.zeros_like(pad_ref)
    for in_ref, out_ref in zip(in_refs, out_refs):
        piece = in_ref.shape[0] - 1
        for b in range(count):
            for h in range(rows):
                at = LINE + b * block + (h + 1) * LINE
                dense = (b * rows + h) * cols
                pad_ref[at : at + cols, :] = in_ref[piece, dense : dense + cols, :]
        for tap in range(9):
            a, c = tap // 3, tap % 3
            pieces = []
            for b in range(count):
                start = LINE + b * block + (2 - a) * LINE - (c - 1)
                pieces.append(pad_ref[start : start + rows * LINE, :])
            high, low = split(jnp.concatenate(pieces, axis=0))
            deep = deep_rows(high, high, low)
            out_ref[tap * LANES : (tap + 1) * LANES, :] = jnp.transpose(deep).astype(
                jnp.bfloat16
            )


def tap_products(shape, chunks, blocks, high, low, w_refs, conv_refs, y_ref):
    count, height, cols = shape
    block = height * LINE
    real = count * block
    high, low = high.astype(jnp.bfloat16), low.astype(jnp.bfloat16)
    for start in range(0, 9 * LANES, 2 * LANES):
        out = slice(start, min(start + 2 * LANES, 9 * LANES))
        lane, product = 0, None
        for ref, chunk in zip(w_refs, chunks):
            lanes = slice(lane, lane + len(chunk) * LANES)
            packed = jnp.concatenate([high[:, lanes], low[:, lanes], high[:, lanes]], axis=1)
            part = dot_nt(packed, ref[out, :])
            product = part if product is None else product + part
            lane += len(chunk) * LANES
        y_ref[:, out] = product
    gap = jnp.zeros((LINE, LANES), jnp.float32)
    for j, conv_ref in enumerate(conv_refs):
        for b in range(count):
            at = j * real + b * block
            sums = []
            for c in range(3):
                above, middle, below = (
                    y_ref[at : at + block, (3 * a + c) * LANES : (3 * a + c + 1) * LANES]
                    for a in range(3)
                )
                sums.append(
                    middle
                    + jnp.concatenate([gap, above[:-LINE]], axis=0)
                    + jnp.concatenate([below[LINE:], gap], axis=0)
                )
            result = (
                sums[1]
                + pltpu.roll(sums[0], 1, axis=0)
                + pltpu.roll(sums[2], block - 1, axis=0)
            )
            for h in range(height):
                dense = (b * height + h) * cols
                conv_ref[dense : dense + cols, :] = result[h * LINE : h * LINE + cols]
        spare = conv_ref.shape[0] - count * height * cols
        if spare:
            conv_ref[count * height * cols :, :] = jnp.zeros((spare, LANES), jnp.float32)


def multiply_kernel(shape, chunks, summed, plan, late, blocks, begun, done, convolve, ids, *refs):
    refs = list(refs)

    def take(k):
        return [refs.pop(0) for _ in range(k)]

    x_refs, g_refs = [take(len(chunks)) for _ in range(blocks)], take(blocks)
    w_refs = take(len(chunks)) if convolve else []
    sum_ref = take(1)[0] if begun is not None else None
    extra_refs = take(len(late)) if done and convolve else []
    conv_refs = take(blocks) if convolve else []
    if done:
        own_ref, mate_ref = take(2)
        extra_out = take(1)[0] if late and not convolve else None
    else:
        (total_ref,) = take(1)
    rows_ref, *y_ref = refs
    count, height, cols = shape
    block = height * LINE
    real = count * block
    first = ids[0] == 0

    rows_ref[...] = jnp.zeros_like(rows_ref)
    for j in range(blocks):
        lane = 0
        for ref, chunk in zip(x_refs[j], chunks):
            for p in range(len(chunk)):
                for line in range(count * height):
                    at = j * real + line * LINE
                    rows_ref[at : at + cols, lane : lane + LANES] = ref[
                        p, line * cols : (line + 1) * cols, :
                    ]
                lane += LANES
    high, low = split(rows_ref[...])

    if convolve:
        tap_products(shape, chunks, blocks, high, low, w_refs, conv_refs, *y_ref)

    places = {pair: (q, i) for q, pairs in enumerate(plan) for i, pair in enumerate(pairs)}
    skip = sum(len(c) for c in chunks if c[0] < summed[0]) * LANES
    lanes = slice(skip, skip + len(summed) * LANES)
    deeps = [
        deep_rows(*(v[j * real : (j + 1) * real, lanes] for v in (high, low, high))).astype(
            jnp.bfloat16
        )
        for j in range(blocks)
    ]

    def keep(owner, at, value):
        slot = slot_of(owner, ids[1], len(plan))
        top, bottom = value[: LANES // CORES], value[LANES // CORES :]
        lanes = slice(at * LANES, (at + 1) * LANES)
        own_ref[slot, :, lanes] = jnp.where(first, top, bottom)
        mate_ref[slot, :, lanes] = jnp.where(first, bottom, top)

    spared = 0
    for tap in range(9):
        out = slice(tap * LANES, (tap + 1) * LANES)
        total = dot_nn(g_refs[0][out, :], deeps[0])
        for j in range(1, blocks):
            total = total + dot_nn(g_refs[j][out, :], deeps[j])
        if begun is not None:
            total = total + sum_ref[out, begun : begun + total.shape[1]]
        if not done:
            total_ref[out, :] = total
            continue
        for p, unit in enumerate(summed):
            value = total[:, p * LANES : (p + 1) * LANES]
            if (tap, unit) in places:
                keep(*places[tap, unit], value)
            else:
                extra_out[spared] = value
                spared += 1
    for ref, pairs in zip(extra_refs, late):
        for i, pair in enumerate(pairs):
            keep(*places[pair], ref[i])


def sum_kernel(plan, width, replicas, ids, *refs):
    *in_refs, out_ref = refs
    span = out_ref.shape[-1]
    for index, owners in enumerate(plan):
        parts = in_refs[index * replicas : (index + 1) * replicas]
        for i in range(len(owners[0])):
            lanes = slice(i * LANES, (i + 1) * LANES)
            value = parts[0][:, lanes]
            for ref in parts[1:]:
                value = value + ref[:, lanes]
            place = jnp.int32(0)
            for q, pairs in enumerate(owners):
                tap, unit = pairs[i]
                place = jnp.where(ids[1] == q, tap * width + unit * LANES - q * span, place)
            out_ref[0, :, pl.ds(pl.multiple_of(place, LANES), LANES)] = value


def on_device(images, filters, out_grad):
    count, rows, cols, chans = images.shape
    owned, kdim = filters.shape[1:]
    width = kdim // 9
    shards, replicas = lax.axis_size("shard"), lax.axis_size("replica")
    parts = shards // CORES
    ups, downs = parts // 2, (parts - 1) // 2
    span = kdim // replicas
    shape = (count, rows, cols)
    real = count * rows * LINE
    packed = -(-count * rows * cols // 8) * 8
    deep = 3 * (real // LANES * LANES) + -(-3 * (real % LANES) // LANES) * LANES
    chunks = chunk_units(width)
    plan = exchange_plan(width, replicas)
    f32 = functools.partial(jax.ShapeDtypeStruct, dtype=jnp.float32)
    bf16 = functools.partial(jax.ShapeDtypeStruct, dtype=jnp.bfloat16)

    ring = list(range(0, parts, 2)) + list(range(1, parts, 2))[::-1]
    table = [
        [s % CORES] + [ring[(ring.index(s // CORES) + d) % parts] for d in range(parts)]
        for s in range(shards)
    ]
    mine = lax.dynamic_index_in_dim(
        jnp.array(table, jnp.int32), lax.axis_index("shard"), 0, keepdims=False
    )
    rep = lax.axis_index("replica").astype(jnp.int32)
    ids = jnp.concatenate([mine[:1], rep[None], mine[1:]])

    def onward(value, d):
        return lax.ppermute(
            value,
            "shard",
            [(s, CORES * table[s][1 + d % parts] + s % CORES) for s in range(shards)],
        )

    def across(value):
        return lax.ppermute(value, "shard", [(s, s ^ 1) for s in range(shards)])

    order = []

    def ordered(kernel, name, out_shape, operands, **keywords):
        first = after(ids, *order[-1:])
        made = call(kernel, name, out_shape, [first, *operands], **keywords)
        order.append(made[0])
        return made

    mate_filters = across(filters)
    size0 = len(chunks[0])
    up, down, *rest, own_grad = ordered(
        functools.partial(pack_kernel, chunks, parts),
        "pack",
        [f32((size0 + n, packed, LANES)) for n in (ups, downs)]
        + [f32((len(c), packed, LANES)) for c in chunks[1:]]
        + [f32((1, packed, LANES))],
        [images, out_grad],
    )

    far = parts - ups
    near = [d for d in range(1, parts) if d != far]
    weights = ordered(
        functools.partial(filter_kernel, chunks),
        "prepare_filters",
        [bf16((9 * LANES, 3 * len(c) * LANES)) for c in chunks],
        [filters, mate_filters],
    )
    pad = [pltpu.VMEM((2 * LINE + count * (rows + 2) * LINE, LANES), jnp.float32)]

    def prepare_grad(blocks):
        return ordered(
            functools.partial(grad_kernel, shape),
            "prepare_grad",
            [bf16((9 * LANES, deep))] * len(blocks),
            blocks,
            scratch=pad,
        )

    def multiply(blocks, grads, summed, begun=None, at=None, late=(), extras=(), done=None, convolve=True):
        units = [chunks[i] for i in (range(len(chunks)) if convolve else summed)]
        lanes = [u for i in summed for u in chunks[i]]
        size = sum(len(c) for c in units) * LANES
        out_shape = [f32((packed, LANES))] * len(blocks) if convolve else []
        if done is None:
            out_shape.append(f32((9 * LANES, len(lanes) * LANES)))
        else:
            out_shape += [f32((replicas, owned, len(plan[done][0]) * LANES))] * 2
            if late and not convolve:
                out_shape.append(f32((len(late), LANES, LANES)))
        operands = [piece for block in blocks for piece in block] + list(grads)
        operands += weights if convolve else []
        operands += [begun] if begun is not None else []
        scratch = [pltpu.VMEM((len(blocks) * real, size), jnp.float32)]
        if convolve:
            scratch.append(pltpu.VMEM((len(blocks) * real, 9 * LANES), jnp.float32))
        made = ordered(
            functools.partial(
                multiply_kernel,
                shape,
                units,
                lanes,
                [] if done is None else plan[done],
                late,
                len(blocks),
                at,
                done is not None,
                convolve,
            ),
            "multiply",
            out_shape,
            operands + list(extras),
            scratch=scratch,
        )
        outputs = len(blocks) if convolve else 0
        return made[:outputs], made[outputs:]

    everything = list(range(len(chunks)))
    grads = [None] * parts
    (grads[0],) = prepare_grad([own_grad])
    (own_conv,), (total,) = multiply([[up, *rest]], grads[:1], everything)

    sent_up, sent_down = [up, *rest], [down, *rest]
    gathered = [None] * parts
    for step in range(1, ups + 1):
        if step <= downs:
            sent_down = [onward(value, -1) for value in sent_down]
            gathered[step] = sent_down
            sent_down = [sent_down[0][:-1], *sent_down[1:]]
        if step < ups:
            sent_up = [onward(value, 1) for value in sent_up]
            gathered[parts - step] = sent_up
            if step + 1 == ups:
                sent_up[0] = after(sent_up[0], total, *sent_up[1:], *sent_down[1:])
            sent_up = [sent_up[0][:-1], *sent_up[1:]]
    near = [d for d in range(1, parts) if d != parts - ups]
    far = parts - ups
    gathered[far] = [onward(sent_up[0], 1)]
    returned = [own_conv] + [None] * (parts - 1)
    if near:
        for d, grad in zip(near, prepare_grad([gathered[d][0] for d in near])):
            grads[d] = grad
        outputs, (total,) = multiply(
            [gathered[d] for d in near], [grads[d] for d in near], everything, total, 0
        )
        for d, value in zip(near, outputs):
            returned[d] = onward(value, d)
        sent_up = sent_up[:1] + [after(value, total) for value in sent_up[1:]]
    gathered[far] += [onward(value, 1) for value in sent_up[1:]]

    (grads[far],) = prepare_grad([gathered[far][0]])
    extras, late, sums = [], [], []
    for index, chunk in enumerate(chunks):
        final = index + 1 == len(chunks)
        carried = {pair for pairs in plan[index] for pair in pairs}
        spare = [(t, u) for t in range(9) for u in chunk if (t, u) not in carried]
        outputs, (own, mate, *spared) = multiply(
            [gathered[far] if final else [gathered[far][index]]],
            [grads[far]],
            [index],
            total,
            chunk[0] * LANES,
            late if final else spare,
            extras if final else (),
            index,
            final,
        )
        if final:
            returned[far] = onward(outputs[0], far)
        extras += spared
        if spare:
            late.append(spare)
        both = own + across(mate)
        sums.append(both[0])
        for step in range(1, replicas):
            sums.append(
                lax.ppermute(
                    both[step],
                    "replica",
                    [(r, partner(r, step, replicas)) for r in range(replicas)],
                )
            )

    (conv_out,) = ordered(
        functools.partial(join_kernel, parts),
        "join_output",
        [f32(images.shape)],
        returned,
    )
    (filter_grad,) = ordered(
        functools.partial(sum_kernel, plan, width, replicas),
        "sum_replicas",
        [f32((1, owned, span))],
        sums,
    )
    return conv_out, filter_grad


def solution(mesh):
    return jax.shard_map(
        on_device,
        mesh=mesh,
        in_specs=(
            P(("replica", "shard"), None, None, None),
            P(None, "shard", None),
            P(("replica", "shard"), None, None, None),
        ),
        out_specs=(P(("replica", "shard"), None, None, None), P(None, "shard", "replica")),
        check_vma=False,
    )
```

```python
import functools

import jax
import jax.numpy as jnp
from jax import lax
from jax.experimental import pallas as pl
from jax.experimental.pallas import tpu as pltpu
from jax.sharding import PartitionSpec as P

CORES = 2
LANES = 128
LINE = 8
CHUNK_SHARES = (2, 2)
VMEM = pl.BlockSpec(memory_space=pltpu.VMEM)


def call(kernel, name, out_shape, operands, scratch=(), mib=24):
    return pl.pallas_call(
        kernel,
        out_shape=out_shape,
        in_specs=[VMEM] * len(operands),
        out_specs=[VMEM] * len(out_shape),
        scratch_shapes=list(scratch),
        compiler_params=pltpu.CompilerParams(vmem_limit_bytes=mib * 1024 * 1024),
        cost_estimate=pl.CostEstimate(flops=0, bytes_accessed=0, transcendentals=0),
        name=name,
    )(*operands)


def ring_of(parts):
    return list(range(0, parts, 2)) + list(range(1, parts, 2))[::-1]


def chip_at(parts, d):
    chip = lax.axis_index("shard") // CORES
    at = jnp.where(chip % 2 == 0, chip // 2, parts - (chip + 1) // 2)
    at = (at + d) % parts
    return jnp.where(at < (parts + 1) // 2, 2 * at, 2 * (parts - at) - 1)


def first_core():
    return lax.axis_index("shard") % CORES == 0


def chunk_units(width):
    units = width // LANES
    share = units // sum(CHUNK_SHARES)
    bounds = [0]
    for part in CHUNK_SHARES:
        bounds.append(bounds[-1] + part * share)
    bounds[-1] = units
    return [list(range(a, b)) for a, b in zip(bounds, bounds[1:])]


def exchange_plan(width, replicas):
    units = width // LANES
    span = 9 * units // replicas
    chunks = chunk_units(width)
    late = [[] for _ in range(replicas)]
    plan = []
    for index, chunk in enumerate(chunks):
        mine = [
            [(t, u) for t in range(9) for u in chunk if (t * units + u) // span == q]
            for q in range(replicas)
        ]
        if index + 1 < len(chunks):
            base = min(len(m) for m in mine)
            for q in range(replicas):
                late[q] += mine[q][base:]
                mine[q] = mine[q][:base]
        else:
            mine = [m + extra for m, extra in zip(mine, late)]
        plan.append(mine)
    return plan


def partner(rep, step, count):
    return (rep + step) % count if count & (count - 1) else rep ^ step


def slot_of(owner, rep, count):
    if count & (count - 1):
        return lax.rem(owner - rep + count, count)
    return jnp.bitwise_xor(jnp.int32(owner), rep)


def after(value, *others):
    return lax.optimization_barrier((value, *others))[0]


def split(value):
    high = value.astype(jnp.bfloat16).astype(jnp.float32)
    return high, value - high


def deep_rows(first, second, third):
    rows, lanes = first.shape
    full = rows // LANES * LANES
    pieces = [p[:full] for p in (first, second, third)] if full else []
    rest = 3 * (rows - full)
    if rest:
        pieces += [p[full:] for p in (first, second, third)]
        gap = -rest % LANES
        if gap:
            pieces.append(jnp.zeros((gap, lanes), jnp.float32))
    return jnp.concatenate(pieces, axis=0)


def dot_nt(lhs, rhs):
    return lax.dot_general(
        lhs, rhs, (((1,), (1,)), ((), ())), preferred_element_type=jnp.float32
    )


def dot_nn(lhs, rhs):
    return lax.dot_general(
        lhs, rhs, (((1,), (0,)), ((), ())), preferred_element_type=jnp.float32
    )


def pack_kernel(parts, image_ref, grad_ref, *refs):
    up_ref, down_ref, *grad_refs = refs
    count, rows, cols, width = image_ref.shape
    dense = count * rows * cols
    units = width // LANES
    spare = up_ref.shape[1] - dense

    def pack(src, lanes, targets):
        for b in range(count):
            for h in range(rows):
                at = (b * rows + h) * cols
                value = src[b, h, :, lanes]
                for ref, p in targets:
                    ref[p, at : at + cols, :] = value
        if spare:
            for ref, p in targets:
                ref[p, dense:, :] = jnp.zeros((spare, LANES), jnp.float32)

    for unit in range(units):
        pack(image_ref, pl.ds(unit * LANES, LANES), [(up_ref, unit), (down_ref, unit)])
    middle = [d for d in range(parts) if d not in (1, parts - 1)]
    for d in range(parts):
        start = pl.multiple_of(chip_at(parts, d) * LANES, LANES)
        if d == 1:
            target = (up_ref, units)
        elif d == parts - 1:
            target = (down_ref, units)
        else:
            target = (grad_refs[middle.index(d)], 0)
        pack(grad_ref, pl.ds(start, LANES), [target])


def join_kernel(parts, *refs):
    out_ref = refs[-1]
    count, rows, cols, width = out_ref.shape
    for d in range(parts):
        start = chip_at(parts, (parts - d) % parts) * LANES
        lanes = pl.ds(pl.multiple_of(start, LANES), LANES)
        for b in range(count):
            for h in range(rows):
                at = (b * rows + h) * cols
                out_ref[b, h, :, lanes] = refs[d][at : at + cols, :]


def filter_kernel(own_ref, mate_ref, out_ref):
    owned, kdim = own_ref.shape[1:]
    width = kdim // 9
    first = first_core()
    for tap in range(9):
        rows = slice(tap * 2 * owned, (tap + 1) * 2 * owned)
        own = own_ref[0, :, tap * width : (tap + 1) * width]
        mate = mate_ref[0, :, tap * width : (tap + 1) * width]
        both = jnp.concatenate(
            [jnp.where(first, own, mate), jnp.where(first, mate, own)], axis=0
        )
        high, low = split(both)
        high = high.astype(jnp.bfloat16)
        out_ref[rows, :width] = high
        out_ref[rows, width : 2 * width] = high
        out_ref[rows, 2 * width :] = low.astype(jnp.bfloat16)


def grad_kernel(shape, *refs):
    count, rows, cols = shape
    *refs, pad_ref = refs
    in_refs, out_refs = refs[: len(refs) // 2], refs[len(refs) // 2 :]
    block = (rows + 2) * LINE
    pad_ref[...] = jnp.zeros_like(pad_ref)
    for in_ref, out_ref in zip(in_refs, out_refs):
        piece = in_ref.shape[0] - 1
        for b in range(count):
            for h in range(rows):
                at = LINE + b * block + (h + 1) * LINE
                dense = (b * rows + h) * cols
                pad_ref[at : at + cols, :] = in_ref[piece, dense : dense + cols, :]
        for tap in range(9):
            a, c = tap // 3, tap % 3
            pieces = []
            for b in range(count):
                start = LINE + b * block + (2 - a) * LINE - (c - 1)
                pieces.append(pad_ref[start : start + rows * LINE, :])
            high, low = split(jnp.concatenate(pieces, axis=0))
            deep = deep_rows(high, high, low)
            out_ref[tap * LANES : (tap + 1) * LANES, :] = jnp.transpose(deep).astype(
                jnp.bfloat16
            )


def tap_products(shape, blocks, high, low, w_ref, conv_refs, y_ref):
    count, height, cols = shape
    block = height * LINE
    real = count * block
    high, low = high.astype(jnp.bfloat16), low.astype(jnp.bfloat16)
    packed = jnp.concatenate([high, low, high], axis=1)
    for start in range(0, 9 * LANES, 2 * LANES):
        out = slice(start, min(start + 2 * LANES, 9 * LANES))
        y_ref[:, out] = dot_nt(packed, w_ref[out, :])
    gap = jnp.zeros((LINE, LANES), jnp.float32)
    for j, conv_ref in enumerate(conv_refs):
        for b in range(count):
            at = j * real + b * block
            sums = []
            for c in range(3):
                above, middle, below = (
                    y_ref[at : at + block, (3 * a + c) * LANES : (3 * a + c + 1) * LANES]
                    for a in range(3)
                )
                sums.append(
                    middle
                    + jnp.concatenate([gap, above[:-LINE]], axis=0)
                    + jnp.concatenate([below[LINE:], gap], axis=0)
                )
            result = (
                sums[1]
                + pltpu.roll(sums[0], 1, axis=0)
                + pltpu.roll(sums[2], block - 1, axis=0)
            )
            for h in range(height):
                dense = (b * height + h) * cols
                conv_ref[dense : dense + cols, :] = result[h * LINE : h * LINE + cols]
        spare = conv_ref.shape[0] - count * height * cols
        if spare:
            conv_ref[count * height * cols :, :] = jnp.zeros((spare, LANES), jnp.float32)


def multiply_kernel(shape, units, blocks, convolve, summed, begun, plan, late, last, *refs):
    refs = list(refs)

    def take(k):
        return [refs.pop(0) for _ in range(k)]

    x_refs = take(blocks)
    w_refs = take(1 if convolve else 0)
    g_refs = take(blocks if summed else 0)
    sum_refs = take(1 if begun is not None else 0)
    extra_refs = take(len(late) if last else 0)
    conv_refs = take(blocks if convolve else 0)
    if plan:
        own_ref, mate_ref = take(2)
        extra_out = take(1)[0] if late and not last else None
    elif summed:
        (total_ref,) = take(1)
    rows_ref, *y_refs = refs
    count, height, cols = shape
    real = count * height * LINE

    rows_ref[...] = jnp.zeros_like(rows_ref)
    for j, ref in enumerate(x_refs):
        for p, unit in enumerate(units):
            for line in range(count * height):
                at = j * real + line * LINE
                rows_ref[at : at + cols, p * LANES : (p + 1) * LANES] = ref[
                    unit, line * cols : (line + 1) * cols, :
                ]
    high, low = split(rows_ref[...])
    if convolve:
        tap_products(shape, blocks, high, low, *w_refs, conv_refs, *y_refs)
    if not summed:
        return

    first = first_core()
    rep = lax.axis_index("replica")
    places = {pair: (q, i) for q, pairs in enumerate(plan) for i, pair in enumerate(pairs)}
    deeps = [
        deep_rows(*(v[j * real : (j + 1) * real] for v in (high, low, high))).astype(jnp.bfloat16)
        for j in range(blocks)
    ]

    def keep(owner, at, value):
        slot = slot_of(owner, rep, len(plan))
        top, bottom = value[: LANES // CORES], value[LANES // CORES :]
        lanes = slice(at * LANES, (at + 1) * LANES)
        own_ref[slot, :, lanes] = jnp.where(first, top, bottom)
        mate_ref[slot, :, lanes] = jnp.where(first, bottom, top)

    spared = 0
    for tap in range(9):
        out = slice(tap * LANES, (tap + 1) * LANES)
        total = dot_nn(g_refs[0][out, :], deeps[0])
        for j in range(1, blocks):
            total = total + dot_nn(g_refs[j][out, :], deeps[j])
        for ref in sum_refs:
            total = total + ref[out, begun : begun + total.shape[1]]
        if not plan:
            total_ref[out, :] = total
            continue
        for p, unit in enumerate(units):
            value = total[:, p * LANES : (p + 1) * LANES]
            if (tap, unit) in places:
                keep(*places[tap, unit], value)
            else:
                extra_out[spared] = value
                spared += 1
    for ref, pairs in zip(extra_refs, late):
        for i, pair in enumerate(pairs):
            keep(*places[pair], ref[i])


def sum_kernel(plan, width, replicas, *refs):
    *in_refs, out_ref = refs
    span = out_ref.shape[-1]
    rep = lax.axis_index("replica")
    for index, owners in enumerate(plan):
        parts = in_refs[index * replicas : (index + 1) * replicas]
        for i in range(len(owners[0])):
            lanes = slice(i * LANES, (i + 1) * LANES)
            value = parts[0][:, lanes]
            for ref in parts[1:]:
                value = value + ref[:, lanes]
            place = jnp.int32(0)
            for q, pairs in enumerate(owners):
                tap, unit = pairs[i]
                place = jnp.where(rep == q, tap * width + unit * LANES - q * span, place)
            out_ref[0, :, pl.ds(pl.multiple_of(place, LANES), LANES)] = value


def on_device(images, filters, out_grad):
    count, rows, cols, chans = images.shape
    owned, kdim = filters.shape[1:]
    width = kdim // 9
    shards, replicas = lax.axis_size("shard"), lax.axis_size("replica")
    parts = shards // CORES
    ups, downs = parts // 2, (parts - 1) // 2
    span = kdim // replicas
    shape = (count, rows, cols)
    real = count * rows * LINE
    packed = -(-count * rows * cols // 8) * 8
    deep = 3 * (real // LANES * LANES) + -(-3 * (real % LANES) // LANES) * LANES
    units = list(range(width // LANES))
    chunks = chunk_units(width)
    plan = exchange_plan(width, replicas)
    f32 = functools.partial(jax.ShapeDtypeStruct, dtype=jnp.float32)
    bf16 = functools.partial(jax.ShapeDtypeStruct, dtype=jnp.bfloat16)
    ring = ring_of(parts)

    def onward(value, d):
        def target(s):
            return CORES * ring[(ring.index(s // CORES) + d) % parts] + s % CORES

        return lax.ppermute(value, "shard", [(s, target(s)) for s in range(shards)])

    def across(value):
        return lax.ppermute(value, "shard", [(s, s ^ 1) for s in range(shards)])

    def to_replica(value, step):
        pairs = [(r, partner(r, step, replicas)) for r in range(replicas)]
        return lax.ppermute(value, "replica", pairs)

    order = []

    def ordered(kernel, name, out_shape, operands, **keywords):
        operands = [after(operands[0], *order[-1:]), *operands[1:]]
        made = call(kernel, name, out_shape, operands, **keywords)
        order.append(made[0])
        return made

    def prepare_grad(blocks):
        return ordered(
            functools.partial(grad_kernel, shape),
            "prepare_grad",
            [bf16((9 * LANES, deep))] * len(blocks),
            blocks,
            scratch=[pltpu.VMEM((2 * LINE + count * (rows + 2) * LINE, LANES), jnp.float32)],
        )

    def multiply(blocks, grads=(), total=None, convolve=True, done=None, late=(), extras=()):
        taken = units if done is None else chunks[done]
        out_shape = [f32((packed, LANES))] * len(blocks) if convolve else []
        last = done is not None and done + 1 == len(chunks)
        if done is not None:
            out_shape += [f32((replicas, owned, len(plan[done][0]) * LANES))] * 2
            if late and not last:
                out_shape.append(f32((len(late), LANES, LANES)))
        elif grads:
            out_shape.append(f32((9 * LANES, width)))
        operands = list(blocks) + ([weights] if convolve else []) + list(grads)
        operands += ([total] if total is not None else []) + list(extras)
        scratch = [pltpu.VMEM((len(blocks) * real, len(taken) * LANES), jnp.float32)]
        if convolve:
            scratch.append(pltpu.VMEM((len(blocks) * real, 9 * LANES), jnp.float32))
        made = ordered(
            functools.partial(
                multiply_kernel,
                shape,
                taken,
                len(blocks),
                convolve,
                bool(grads),
                None if total is None else taken[0] * LANES,
                [] if done is None else plan[done],
                late,
                last,
            ),
            "multiply",
            out_shape,
            operands,
            scratch=scratch,
        )
        outputs = len(blocks) if convolve else 0
        return made[:outputs], made[outputs:]

    mate_filters = across(filters)
    middle = [d for d in range(parts) if d not in (1, parts - 1)]
    up, down, *split_grads = ordered(
        functools.partial(pack_kernel, parts),
        "pack",
        [f32((len(units) + 1, packed, LANES))] * 2 + [f32((1, packed, LANES))] * len(middle),
        [images, out_grad],
    )
    grad_blocks = [None] * parts
    grad_blocks[0] = split_grads[0]
    for d, value in zip(middle[1:], split_grads[1:]):
        grad_blocks[parts - d] = onward(value, d)
    (weights,) = ordered(
        filter_kernel,
        "prepare_filters",
        [bf16((9 * LANES, 3 * width))],
        [filters, mate_filters],
    )
    grads = [None] * parts
    for d, grad in zip(middle, prepare_grad([grad_blocks[d] for d in middle])):
        grads[d] = grad
    (own_conv,), (total,) = multiply([up], grads[:1])

    blocks = [up] + [None] * (parts - 1)
    for step in range(1, ups + 1):
        up = onward(up, 1)
        blocks[parts - step] = up
        if step <= downs:
            down = onward(down, -1)
            blocks[step] = down
        if step == 1:
            up = after(up, total)
        up, down = up[: len(units)], down[: len(units)]
    far = parts - ups
    near = [d for d in range(1, parts) if d != far]
    ends = [d for d in (1, parts - 1) if grads[d] is None]
    for d, grad in zip(ends, prepare_grad([blocks[d] for d in ends])):
        grads[d] = grad
    returned = [own_conv] + [None] * (parts - 1)
    outputs, (total,) = multiply([blocks[d] for d in near], [grads[d] for d in near], total)
    for d, value in zip(near, outputs):
        returned[d] = value

    extras, late, sums, previous = [], [], [], []
    for index, chunk in enumerate(chunks):
        last = index + 1 == len(chunks)
        carried = {pair for pairs in plan[index] for pair in pairs}
        spare = [(t, u) for t in range(9) for u in chunk if (t, u) not in carried]
        _, (own, mate, *spared) = multiply(
            [blocks[far]],
            [grads[far]],
            total,
            convolve=False,
            done=index,
            late=late if last else spare,
            extras=extras if last else (),
        )
        extras += spared
        if spare:
            late.append(spare)
        both = own + across(mate)
        sums.append(both[0])
        arrived = []
        for step in range(1, replicas):
            value = both[step]
            if previous:
                value = after(value, previous[step - 1])
            arrived.append(to_replica(value, step))
        sums += arrived
        if last:
            order.append(both)
            (returned[far],), _ = multiply([blocks[far]])
            settled = previous[-1:]
        previous = arrived
    for d in near + [far]:
        returned[d] = onward(after(returned[d], *settled), d)

    (conv_out,) = ordered(
        functools.partial(join_kernel, parts),
        "join_output",
        [f32(images.shape)],
        returned,
    )
    (filter_grad,) = ordered(
        functools.partial(sum_kernel, plan, width, replicas),
        "sum_replicas",
        [f32((1, owned, span))],
        sums,
    )
    return conv_out, filter_grad


def solution(mesh):
    return jax.shard_map(
        on_device,
        mesh=mesh,
        in_specs=(
            P(("replica", "shard"), None, None, None),
            P(None, "shard", None),
            P(("replica", "shard"), None, None, None),
        ),
        out_specs=(P(("replica", "shard"), None, None, None), P(None, "shard", "replica")),
        check_vma=False,
    )
```

```python
import functools

import jax
import jax.numpy as jnp
from jax import lax
from jax.experimental import pallas as pl
from jax.experimental.pallas import tpu as pltpu
from jax.sharding import PartitionSpec as P

CORES = 2
LANES = 128
LINE = 8
CHUNK_SHARES = (2, 2)
VMEM = pl.BlockSpec(memory_space=pltpu.VMEM)


def call(kernel, name, out_shape, operands, scratch=(), mib=24):
    return pl.pallas_call(
        kernel,
        out_shape=out_shape,
        in_specs=[VMEM] * len(operands),
        out_specs=[VMEM] * len(out_shape),
        scratch_shapes=list(scratch),
        compiler_params=pltpu.CompilerParams(vmem_limit_bytes=mib * 1024 * 1024),
        cost_estimate=pl.CostEstimate(flops=0, bytes_accessed=0, transcendentals=0),
        name=name,
    )(*operands)


def ring_of(parts):
    return list(range(0, parts, 2)) + list(range(1, parts, 2))[::-1]


def chip_at(parts, d):
    chip = lax.axis_index("shard") // CORES
    at = jnp.where(chip % 2 == 0, chip // 2, parts - (chip + 1) // 2)
    at = (at + d) % parts
    return jnp.where(at < (parts + 1) // 2, 2 * at, 2 * (parts - at) - 1)


def first_core():
    return lax.axis_index("shard") % CORES == 0


def chunk_units(width):
    units = width // LANES
    share = units // sum(CHUNK_SHARES)
    bounds = [0]
    for part in CHUNK_SHARES:
        bounds.append(bounds[-1] + part * share)
    bounds[-1] = units
    return [list(range(a, b)) for a, b in zip(bounds, bounds[1:])]


def exchange_plan(width, replicas):
    units = width // LANES
    span = 9 * units // replicas
    chunks = chunk_units(width)
    late = [[] for _ in range(replicas)]
    plan = []
    for index, chunk in enumerate(chunks):
        mine = [
            [(t, u) for t in range(9) for u in chunk if (t * units + u) // span == q]
            for q in range(replicas)
        ]
        if index + 1 < len(chunks):
            base = min(len(m) for m in mine)
            for q in range(replicas):
                late[q] += mine[q][base:]
                mine[q] = mine[q][:base]
        else:
            mine = [m + extra for m, extra in zip(mine, late)]
        plan.append(mine)
    return plan


def partner(rep, step, count):
    return (rep + step) % count if count & (count - 1) else rep ^ step


def slot_of(owner, rep, count):
    if count & (count - 1):
        return lax.rem(owner - rep + count, count)
    return jnp.bitwise_xor(jnp.int32(owner), rep)


def after(value, *others):
    return lax.optimization_barrier((value, *others))[0]


def split(value):
    high = value.astype(jnp.bfloat16).astype(jnp.float32)
    return high, value - high


def deep_rows(first, second, third):
    rows, lanes = first.shape
    full = rows // LANES * LANES
    pieces = [p[:full] for p in (first, second, third)] if full else []
    rest = 3 * (rows - full)
    if rest:
        pieces += [p[full:] for p in (first, second, third)]
        gap = -rest % LANES
        if gap:
            pieces.append(jnp.zeros((gap, lanes), jnp.float32))
    return jnp.concatenate(pieces, axis=0)


def dot_nt(lhs, rhs):
    return lax.dot_general(
        lhs, rhs, (((1,), (1,)), ((), ())), preferred_element_type=jnp.float32
    )


def dot_nn(lhs, rhs):
    return lax.dot_general(
        lhs, rhs, (((1,), (0,)), ((), ())), preferred_element_type=jnp.float32
    )


def pack_kernel(parts, image_ref, grad_ref, ring_ref, own_ref, back_ref):
    count, rows, cols, width = image_ref.shape
    dense = count * rows * cols
    units = width // LANES
    spare = ring_ref.shape[1] - dense

    def pack(src, lanes, ref, p):
        for b in range(count):
            for h in range(rows):
                at = (b * rows + h) * cols
                ref[p, at : at + cols, :] = src[b, h, :, lanes]
        if spare:
            ref[p, dense:, :] = jnp.zeros((spare, LANES), jnp.float32)

    for unit in range(units):
        pack(image_ref, pl.ds(unit * LANES, LANES), ring_ref, unit)
    for d in range(parts):
        lanes = pl.ds(pl.multiple_of(chip_at(parts, d) * LANES, LANES), LANES)
        if d == 0:
            pack(grad_ref, lanes, own_ref, 0)
        elif d == parts - 1:
            pack(grad_ref, lanes, back_ref, 0)
        else:
            pack(grad_ref, lanes, ring_ref, ring_ref.shape[0] - d)


def join_kernel(parts, *refs):
    out_ref = refs[-1]
    count, rows, cols, width = out_ref.shape
    for d in range(parts):
        start = chip_at(parts, (parts - d) % parts) * LANES
        lanes = pl.ds(pl.multiple_of(start, LANES), LANES)
        for b in range(count):
            for h in range(rows):
                at = (b * rows + h) * cols
                out_ref[b, h, :, lanes] = refs[d][at : at + cols, :]


def filter_kernel(own_ref, mate_ref, out_ref):
    owned, kdim = own_ref.shape[1:]
    width = kdim // 9
    first = first_core()
    for tap in range(9):
        rows = slice(tap * 2 * owned, (tap + 1) * 2 * owned)
        own = own_ref[0, :, tap * width : (tap + 1) * width]
        mate = mate_ref[0, :, tap * width : (tap + 1) * width]
        both = jnp.concatenate(
            [jnp.where(first, own, mate), jnp.where(first, mate, own)], axis=0
        )
        high, low = split(both)
        high = high.astype(jnp.bfloat16)
        out_ref[rows, :width] = high
        out_ref[rows, width : 2 * width] = high
        out_ref[rows, 2 * width :] = low.astype(jnp.bfloat16)


def grad_kernel(shape, *refs):
    count, rows, cols = shape
    *refs, pad_ref = refs
    in_refs, out_refs = refs[: len(refs) // 2], refs[len(refs) // 2 :]
    block = (rows + 2) * LINE
    pad_ref[...] = jnp.zeros_like(pad_ref)
    for in_ref, out_ref in zip(in_refs, out_refs):
        piece = in_ref.shape[0] - 1
        for b in range(count):
            for h in range(rows):
                at = LINE + b * block + (h + 1) * LINE
                dense = (b * rows + h) * cols
                pad_ref[at : at + cols, :] = in_ref[piece, dense : dense + cols, :]
        for tap in range(9):
            a, c = tap // 3, tap % 3
            pieces = []
            for b in range(count):
                start = LINE + b * block + (2 - a) * LINE - (c - 1)
                pieces.append(pad_ref[start : start + rows * LINE, :])
            high, low = split(jnp.concatenate(pieces, axis=0))
            deep = deep_rows(high, high, low)
            out_ref[tap * LANES : (tap + 1) * LANES, :] = jnp.transpose(deep).astype(
                jnp.bfloat16
            )


def tap_products(shape, blocks, high, low, w_ref, conv_refs, y_ref):
    count, height, cols = shape
    block = height * LINE
    real = count * block
    high, low = high.astype(jnp.bfloat16), low.astype(jnp.bfloat16)
    packed = jnp.concatenate([high, low, high], axis=1)
    for start in range(0, 9 * LANES, 2 * LANES):
        out = slice(start, min(start + 2 * LANES, 9 * LANES))
        y_ref[:, out] = dot_nt(packed, w_ref[out, :])
    gap = jnp.zeros((LINE, LANES), jnp.float32)
    for j, conv_ref in enumerate(conv_refs):
        for b in range(count):
            at = j * real + b * block
            sums = []
            for c in range(3):
                above, middle, below = (
                    y_ref[at : at + block, (3 * a + c) * LANES : (3 * a + c + 1) * LANES]
                    for a in range(3)
                )
                sums.append(
                    middle
                    + jnp.concatenate([gap, above[:-LINE]], axis=0)
                    + jnp.concatenate([below[LINE:], gap], axis=0)
                )
            result = (
                sums[1]
                + pltpu.roll(sums[0], 1, axis=0)
                + pltpu.roll(sums[2], block - 1, axis=0)
            )
            for h in range(height):
                dense = (b * height + h) * cols
                conv_ref[dense : dense + cols, :] = result[h * LINE : h * LINE + cols]
        spare = conv_ref.shape[0] - count * height * cols
        if spare:
            conv_ref[count * height * cols :, :] = jnp.zeros((spare, LANES), jnp.float32)


def multiply_kernel(shape, units, blocks, convolve, summed, begun, plan, late, last, *refs):
    refs = list(refs)

    def take(k):
        return [refs.pop(0) for _ in range(k)]

    x_refs = take(blocks)
    w_refs = take(1 if convolve else 0)
    g_refs = take(blocks if summed else 0)
    sum_refs = take(1 if begun is not None else 0)
    extra_refs = take(len(late) if last else 0)
    conv_refs = take(blocks if convolve else 0)
    if plan:
        own_ref, mate_ref = take(2)
        extra_out = take(1)[0] if late and not last else None
    elif summed:
        (total_ref,) = take(1)
    rows_ref, *y_refs = refs
    count, height, cols = shape
    real = count * height * LINE

    rows_ref[...] = jnp.zeros_like(rows_ref)
    for j, ref in enumerate(x_refs):
        for p, unit in enumerate(units):
            for line in range(count * height):
                at = j * real + line * LINE
                rows_ref[at : at + cols, p * LANES : (p + 1) * LANES] = ref[
                    unit, line * cols : (line + 1) * cols, :
                ]
    high, low = split(rows_ref[...])
    if convolve:
        tap_products(shape, blocks, high, low, *w_refs, conv_refs, *y_refs)
    if not summed:
        return

    first = first_core()
    rep = lax.axis_index("replica")
    places = {pair: (q, i) for q, pairs in enumerate(plan) for i, pair in enumerate(pairs)}
    deeps = [
        deep_rows(*(v[j * real : (j + 1) * real] for v in (high, low, high))).astype(jnp.bfloat16)
        for j in range(blocks)
    ]

    def keep(owner, at, value):
        slot = slot_of(owner, rep, len(plan))
        top, bottom = value[: LANES // CORES], value[LANES // CORES :]
        lanes = slice(at * LANES, (at + 1) * LANES)
        own_ref[slot, :, lanes] = jnp.where(first, top, bottom)
        mate_ref[slot, :, lanes] = jnp.where(first, bottom, top)

    spared = 0
    for tap in range(9):
        out = slice(tap * LANES, (tap + 1) * LANES)
        total = dot_nn(g_refs[0][out, :], deeps[0])
        for j in range(1, blocks):
            total = total + dot_nn(g_refs[j][out, :], deeps[j])
        for ref in sum_refs:
            total = total + ref[out, begun : begun + total.shape[1]]
        if not plan:
            total_ref[out, :] = total
            continue
        for p, unit in enumerate(units):
            value = total[:, p * LANES : (p + 1) * LANES]
            if (tap, unit) in places:
                keep(*places[tap, unit], value)
            else:
                extra_out[spared] = value
                spared += 1
    for ref, pairs in zip(extra_refs, late):
        for i, pair in enumerate(pairs):
            keep(*places[pair], ref[i])


def sum_kernel(plan, width, replicas, *refs):
    *in_refs, out_ref = refs
    span = out_ref.shape[-1]
    rep = lax.axis_index("replica")
    for index, owners in enumerate(plan):
        parts = in_refs[index * replicas : (index + 1) * replicas]
        for i in range(len(owners[0])):
            lanes = slice(i * LANES, (i + 1) * LANES)
            value = parts[0][:, lanes]
            for ref in parts[1:]:
                value = value + ref[:, lanes]
            place = jnp.int32(0)
            for q, pairs in enumerate(owners):
                tap, unit = pairs[i]
                place = jnp.where(rep == q, tap * width + unit * LANES - q * span, place)
            out_ref[0, :, pl.ds(pl.multiple_of(place, LANES), LANES)] = value


def on_device(images, filters, out_grad):
    count, rows, cols, chans = images.shape
    owned, kdim = filters.shape[1:]
    width = kdim // 9
    shards, replicas = lax.axis_size("shard"), lax.axis_size("replica")
    parts = shards // CORES
    span = kdim // replicas
    shape = (count, rows, cols)
    real = count * rows * LINE
    packed = -(-count * rows * cols // 8) * 8
    deep = 3 * (real // LANES * LANES) + -(-3 * (real % LANES) // LANES) * LANES
    units = list(range(width // LANES))
    chunks = chunk_units(width)
    plan = exchange_plan(width, replicas)
    f32 = functools.partial(jax.ShapeDtypeStruct, dtype=jnp.float32)
    bf16 = functools.partial(jax.ShapeDtypeStruct, dtype=jnp.bfloat16)
    ring = ring_of(parts)

    def onward(value, d):
        def target(s):
            return CORES * ring[(ring.index(s // CORES) + d) % parts] + s % CORES

        return lax.ppermute(value, "shard", [(s, target(s)) for s in range(shards)])

    def across(value):
        return lax.ppermute(value, "shard", [(s, s ^ 1) for s in range(shards)])

    def to_replica(value, step):
        pairs = [(r, partner(r, step, replicas)) for r in range(replicas)]
        return lax.ppermute(value, "replica", pairs)

    order = []

    def ordered(kernel, name, out_shape, operands, **keywords):
        operands = [after(operands[0], *order[-1:]), *operands[1:]]
        made = call(kernel, name, out_shape, operands, **keywords)
        order.append(made[0])
        return made

    def prepare_grad(blocks):
        return ordered(
            functools.partial(grad_kernel, shape),
            "prepare_grad",
            [bf16((9 * LANES, deep))] * len(blocks),
            blocks,
            scratch=[pltpu.VMEM((2 * LINE + count * (rows + 2) * LINE, LANES), jnp.float32)],
        )

    def multiply(blocks, grads=(), total=None, convolve=True, done=None, late=(), extras=()):
        taken = units if done is None else chunks[done]
        out_shape = [f32((packed, LANES))] * len(blocks) if convolve else []
        last = done is not None and done + 1 == len(chunks)
        if done is not None:
            out_shape += [f32((replicas, owned, len(plan[done][0]) * LANES))] * 2
            if late and not last:
                out_shape.append(f32((len(late), LANES, LANES)))
        elif grads:
            out_shape.append(f32((9 * LANES, width)))
        operands = list(blocks) + ([weights] if convolve else []) + list(grads)
        operands += ([total] if total is not None else []) + list(extras)
        scratch = [pltpu.VMEM((len(blocks) * real, len(taken) * LANES), jnp.float32)]
        if convolve:
            scratch.append(pltpu.VMEM((len(blocks) * real, 9 * LANES), jnp.float32))
        made = ordered(
            functools.partial(
                multiply_kernel,
                shape,
                taken,
                len(blocks),
                convolve,
                bool(grads),
                None if total is None else taken[0] * LANES,
                [] if done is None else plan[done],
                late,
                last,
            ),
            "multiply",
            out_shape,
            operands,
            scratch=scratch,
        )
        outputs = len(blocks) if convolve else 0
        return made[:outputs], made[outputs:]

    mate_filters = across(filters)
    passing, own_grad, back_grad = ordered(
        functools.partial(pack_kernel, parts),
        "pack",
        [f32((len(units) + parts - 2, packed, LANES))] + [f32((1, packed, LANES))] * 2,
        [images, out_grad],
    )
    far_grad = onward(back_grad, -1)
    (weights,) = ordered(
        filter_kernel,
        "prepare_filters",
        [bf16((9 * LANES, 3 * width))],
        [filters, mate_filters],
    )
    grad, last_grad = prepare_grad([own_grad, far_grad])
    (own_conv,), (total,) = multiply([passing], [grad])

    outputs = {0: own_conv}
    for step in range(1, parts):
        passing = onward(passing, 1)
        if step + 1 < parts:
            passing = after(passing, total)
        if step + 1 == parts:
            break
        (grad,) = prepare_grad([passing])
        (outputs[parts - step],), (total,) = multiply([passing], [grad], total)
        passing = passing[:-1]
    far = 1

    extras, late, sums, previous = [], [], [], []
    for index, chunk in enumerate(chunks):
        last = index + 1 == len(chunks)
        carried = {pair for pairs in plan[index] for pair in pairs}
        spare = [(t, u) for t in range(9) for u in chunk if (t, u) not in carried]
        _, (own, mate, *spared) = multiply(
            [passing],
            [last_grad],
            total,
            convolve=False,
            done=index,
            late=late if last else spare,
            extras=extras if last else (),
        )
        extras += spared
        if spare:
            late.append(spare)
        both = own + across(mate)
        sums.append(both[0])
        arrived = []
        for step in range(1, replicas):
            value = both[step]
            if previous and step == 1:
                value = after(value, previous[-1])
            arrived.append(to_replica(value, step))
        sums += arrived
        if last:
            order.append(both)
        else:
            previous = arrived
    (outputs[far],), _ = multiply([passing])

    waits = (previous[:-1][::-1] + arrived[::-1])[: parts - 1]
    waits += [waits[-1]] * (parts - 1 - len(waits))
    returned = [own_conv] + [None] * (parts - 1)
    for d, earlier in zip(sorted(set(range(1, parts)) - {far}) + [far], waits):
        returned[d] = onward(after(outputs[d], earlier), d)

    (conv_out,) = ordered(
        functools.partial(join_kernel, parts),
        "join_output",
        [f32(images.shape)],
        returned,
    )
    (filter_grad,) = ordered(
        functools.partial(sum_kernel, plan, width, replicas),
        "sum_replicas",
        [f32((1, owned, span))],
        sums,
    )
    return conv_out, filter_grad


def solution(mesh):
    return jax.shard_map(
        on_device,
        mesh=mesh,
        in_specs=(
            P(("replica", "shard"), None, None, None),
            P(None, "shard", None),
            P(("replica", "shard"), None, None, None),
        ),
        out_specs=(P(("replica", "shard"), None, None, None), P(None, "shard", "replica")),
        check_vma=False,
    )
```
